256 devices in a mesh: dp: 2 (over core), row: 8 (over z), col: 16 (over y, x).
Axes of the slice: x: 4, y: 4, z: 8, core: 2. Of those that a mesh axis runs over, the one named last changes fastest.
Arguments:
- tokens: bfloat16 [1024, 8192], P(('dp', 'row'), 'col'), may hold values from -6 to 6
- cotangent: bfloat16 [1024, 8192], P(('dp', 'row'), 'col'), may hold values from -1.5 to 1.5
- gate_weight: bfloat16 [8192, 14336], P('col', 'row'), may hold values from -0.0625 to 0.0625
- up_weight: bfloat16 [8192, 14336], P('col', 'row'), may hold values from -0.0625 to 0.0625
- down_weight: bfloat16 [14336, 8192], P('row', 'col'), may hold values from -0.046875 to 0.046875
Outputs:
- input_grad: bfloat16 [1024, 8192], P(('dp', 'row'), 'col')
- gate_wgrad: bfloat16 [8192, 14336], P('col', 'row')
- up_wgrad: bfloat16 [8192, 14336], P('col', 'row')
- down_wgrad: bfloat16 [14336, 8192], P('row', 'col')
The draws below stay inside these ranges and needn't reach their ends.
All inputs are finite; a program needn't handle non-finite values.
Results may differ from the reference program's by a relative error of at most 0.033.
Values may be sent and summed in bfloat16 or wider, within the bound.
No kernel may reach another device: no remote copies, remote signals or barrier semaphores. Data moves between devices by JAX's collectives and lax.ppermute only.
A program may use at most 128 MiB of HBM per device.

```python
import jax
import jax.numpy as jnp
from jax import lax

D = 8192
FF = 14336
TOK = 512
TOKENS = 1024
N_DP = 2
N_ROW = 8
N_COL = 16


def block_levels(own_key, shape, pieces, smallest, largest):
    level = 1.0
    for position, parts in pieces:
        heights = jax.random.uniform(jax.random.fold_in(jax.random.fold_in(own_key, 6), position), (parts,), jnp.float32, smallest / len(pieces), largest / len(pieces))
        level = level * jnp.repeat(jnp.exp(heights), shape[position] // parts).reshape((-1,) + (1,) * (len(shape) - 1 - position))
    return level


def normal_values(rng, shape, scale, bound, pieces=(), kind=jnp.bfloat16):
    values = jax.random.normal(rng, shape, jnp.float32) * scale
    if len(pieces) > 0:
        values = block_levels(rng, shape, pieces, -0.22, 0.18) * values
    return jnp.clip(values, min=-bound, max=bound).astype(kind)


def setup_inputs(seed: int = 0) -> dict:
    keys = jax.random.split(jax.random.key(seed), 6)
    tokens = normal_values(keys[0], (TOKENS, D), 1.0, 6.0, ((0, 16), (1, 16)))
    cotangent = normal_values(keys[1], (TOKENS, D), 0.25, 1.5, ((0, 16), (1, 16)))
    gate_weight = normal_values(keys[2], (D, FF), D ** -0.5, 0.0625, ((0, 16), (1, 8)))
    up_weight = normal_values(keys[3], (D, FF), D ** -0.5, 0.0625, ((0, 16), (1, 8)))
    down_weight = normal_values(keys[4], (FF, D), FF ** -0.5, 0.046875, ((0, 8), (1, 16)))
    return {"tokens": tokens, "cotangent": cotangent, "gate_weight": gate_weight, "up_weight": up_weight, "down_weight": down_weight}


def rounded(values):
    return lax.optimization_barrier(values.astype(jnp.bfloat16)).astype(jnp.float32)


def block_sum(left, right, blocks):
    width = left.shape[1] // blocks
    total = jnp.zeros((left.shape[0], right.shape[1]), jnp.float32)
    for block in range(blocks):
        partial_value = jnp.dot(left[:, block * width:(block + 1) * width], right[block * width:(block + 1) * width],
                          preferred_element_type=jnp.float32)
        total = total + rounded(partial_value)
    return total


def input_sum(gate_grad, up_grad, gate_weight, up_weight, blocks):
    width = gate_grad.shape[1] // blocks
    total = jnp.zeros((gate_grad.shape[0], gate_weight.shape[0]), jnp.float32)
    for block in range(blocks):
        lower = block * width
        upper = lower + width
        partial_value = jnp.dot(gate_grad[:, lower:upper], gate_weight[:, lower:upper].T, preferred_element_type=jnp.float32)
        partial_value = partial_value + jnp.dot(up_grad[:, lower:upper], up_weight[:, lower:upper].T, preferred_element_type=jnp.float32)
        total = total + rounded(partial_value)
    return total


def reference(tokens, cotangent, gate_weight, up_weight, down_weight):
    totals = None
    grad_blocks = []
    for replica in range(N_DP):
        in_rows = tokens[replica * TOK:(replica + 1) * TOK]
        up_rows = cotangent[replica * TOK:(replica + 1) * TOK]
        gate_sum = block_sum(in_rows, gate_weight, N_COL)
        up_sum = block_sum(in_rows, up_weight, N_COL)
        back_sum = block_sum(up_rows, down_weight.T, N_COL)
        sigmoid_gate = jax.nn.sigmoid(gate_sum)
        hidden = (gate_sum * sigmoid_gate * up_sum).astype(jnp.bfloat16)
        gate_grad = (back_sum * up_sum * sigmoid_gate * (1.0 + gate_sum * (1.0 - sigmoid_gate))).astype(jnp.bfloat16)
        up_grad = (back_sum * gate_sum * sigmoid_gate).astype(jnp.bfloat16)
        block_grad = input_sum(gate_grad, up_grad, gate_weight, up_weight, N_ROW)
        grad_blocks.append(block_grad.astype(jnp.bfloat16))
        terms = (rounded(jnp.dot(in_rows.T, gate_grad, preferred_element_type=jnp.float32)),
                 rounded(jnp.dot(in_rows.T, up_grad, preferred_element_type=jnp.float32)),
                 rounded(jnp.dot(hidden.T, up_rows, preferred_element_type=jnp.float32)))
        if totals is None:
            totals = terms
        else:
            totals = (totals[0] + terms[0], totals[1] + terms[1], totals[2] + terms[2])
    input_grad = jnp.concatenate(grad_blocks, axis=0)
    return (input_grad, totals[0].astype(jnp.bfloat16), totals[1].astype(jnp.bfloat16),
            totals[2].astype(jnp.bfloat16))
```

```python
import functools

import jax
import jax.numpy as jnp
from jax import lax
from jax.experimental import pallas as pl
from jax.experimental.pallas import tpu as pltpu
from jax.sharding import PartitionSpec as P

RING = 4
BF16 = jnp.bfloat16
F32 = jnp.float32
VMEM_LIMIT = 56 * 1024 * 1024


def col_shift(axis, step):
    pairs = []
    for y in range(RING):
        for x in range(RING):
            if axis == 0:
                to = y * RING + (x + step) % RING
            else:
                to = ((y + step) % RING) * RING + x
            pairs.append((y * RING + x, to))
    return pairs


def send_col(value, axis, step):
    return lax.ppermute(value, "col", col_shift(axis, step))


def send_row(value, step):
    return lax.ppermute(value, "row", [(i, (i + step) % 8) for i in range(8)])


def swap_dp(value):
    return lax.ppermute(value, "dp", [(0, 1), (1, 0)])


def call(kernel, outs, args, scratch=(), flops=0):
    whole = pl.BlockSpec(memory_space=pltpu.VMEM)
    small = pl.BlockSpec(memory_space=pltpu.SMEM)
    moved = sum(a.size * a.dtype.itemsize for a in args)
    return pl.pallas_call(
        kernel,
        out_shape=[jax.ShapeDtypeStruct(shape, kind) for shape, kind in outs],
        in_specs=[small if a.dtype == jnp.int32 else whole for a in args],
        out_specs=[whole] * len(outs),
        scratch_shapes=list(scratch),
        compiler_params=pltpu.CompilerParams(vmem_limit_bytes=VMEM_LIMIT),
        cost_estimate=pl.CostEstimate(flops=flops, bytes_accessed=moved, transcendentals=0),
    )(*args)


def rows_of(start, count):
    return pl.ds(pl.multiple_of(start, 32), count)


def three_products(act, weights, half, slices):
    gate, up, down = weights
    width = gate.shape[0]
    hid = gate.shape[1] // 2
    cols = slice(half * hid, (half + 1) * hid)
    tok = [act[s, :width] for s in slices]
    cot = [act[s, width:] for s in slices]
    tok = tok[0] if len(tok) == 1 else jnp.concatenate(tok, axis=0)
    cot = cot[0] if len(cot) == 1 else jnp.concatenate(cot, axis=0)
    return (
        jnp.dot(tok, gate[:, cols], preferred_element_type=F32),
        jnp.dot(tok, up[:, cols], preferred_element_type=F32),
        lax.dot_general(
            cot, down[cols, :], (((1,), (1,)), ((), ())), preferred_element_type=F32
        ),
    )


def far_kernel(place, act, gate, up, down, *outs):
    for half in range(2):
        here = place[half]
        block = lax.rem(here + 2, RING) * 128
        terms = three_products(act, (gate, up, down), half, [rows_of(block, 128)])
        for k in range(3):
            outs[2 * half][k] = terms[k][:64].astype(BF16)
            outs[2 * half + 1][k] = terms[k][64:].astype(BF16)


def near_kernel(place, act, gate, up, down, *outs):
    for half in range(2):
        here = place[half]
        after = lax.rem(here + 1, RING) * 128 + 64
        before = lax.rem(here + 3, RING) * 128
        terms = three_products(
            act, (gate, up, down), half, [rows_of(after, 64), rows_of(before, 64)]
        )
        for k in range(3):
            outs[2 * half][k] = terms[k][:64].astype(BF16)
            outs[2 * half + 1][k] = terms[k][64:].astype(BF16)


def relay_kernel(place, act, gate, up, down, r0, r1, r2, r3, *outs):
    got = (r0, r1, r2, r3)
    for half in range(2):
        here = place[half]
        after = lax.rem(here + 1, RING) * 128
        before = lax.rem(here + 3, RING) * 128 + 64
        terms = three_products(
            act, (gate, up, down), half, [rows_of(after, 64), rows_of(before, 64)]
        )
        for k in range(3):
            outs[2 * half][k] = (terms[k][:64] + got[2 * half][k].astype(F32)).astype(BF16)
            outs[2 * half + 1][k] = (terms[k][64:] + got[2 * half + 1][k].astype(F32)).astype(BF16)


def own_kernel(place, act, gate, up, down, *refs):
    got, outs, held = refs[:8], refs[8:16], refs[16]
    for half in range(2):
        here, other = place[half], place[1 - half]
        near_up, near_down, relay_up, relay_down = got[4 * half : 4 * half + 4]
        terms = three_products(act, (gate, up, down), half, [rows_of(here * 128, 128)])
        for k in range(3):
            held[k, :64] = terms[k][:64] + relay_up[k].astype(F32) + near_down[k].astype(F32)
            held[k, 64:] = terms[k][64:] + relay_down[k].astype(F32) + near_up[k].astype(F32)
        for step in range(RING):
            rows = rows_of(lax.rem(other + step, RING) * 32, 32)
            out = outs[4 * half + step]
            for k in range(3):
                out[k] = held[k, rows, :].astype(out.dtype)


def unit_kernel(*refs):
    for half in range(2):
        own, one, two, three = refs[4 * half : 4 * half + 4]
        out = refs[8 + half]
        gate_sum, up_sum, back_sum = (
            own[k] + one[k].astype(F32) + two[k].astype(F32) + three[k].astype(F32)
            for k in range(3)
        )
        sig = jax.nn.sigmoid(gate_sum)
        silu = gate_sum * sig
        out[0] = (back_sum * up_sum * sig * (1.0 + gate_sum * (1.0 - sig))).astype(BF16)
        out[1] = (back_sum * silu).astype(BF16)
        out[2] = (silu * up_sum).astype(BF16)


def join_kernel(*refs):
    for half in range(2):
        parts = refs[4 * half : 4 * half + 4]
        for k in range(3):
            for j in range(4):
                out = refs[8 + 2 * half + j // 2]
                out[k, 32 * (j % 2) : 32 * (j % 2) + 32, :] = parts[j][k]


def assemble(place, pieces, kinds, targets):
    hid = pieces[0].shape[2]
    for half in range(2):
        here, other = place[half], place[1 - half]
        for block, step in enumerate((0, 3, 1, 2)):
            base = lax.rem(here + step, RING) * 128
            for j in range(4):
                piece = pieces[8 * half + 2 * block + j // 2]
                rows = rows_of(base + lax.rem(other + RING - j, RING) * 32, 32)
                lower = 32 * (j % 2)
                for k, target in zip(kinds, targets):
                    target[rows, half * hid : (half + 1) * hid] = piece[k, lower : lower + 32, :]


def input_kernel(place, gate, up, *refs):
    pieces, outs, (gg, ug) = refs[:16], refs[16:24], refs[24:]
    assemble(place, pieces, (0, 1), (gg, ug))
    contract = (((1,), (1,)), ((), ()))
    for part in range(8):
        rows = slice(64 * part, 64 * part + 64)
        if part % 4 == 0:
            wide = slice(64 * part, 64 * part + 256)
            total = lax.dot_general(gg[wide], gate[...], contract, preferred_element_type=F32)
            total += lax.dot_general(ug[wide], up[...], contract, preferred_element_type=F32)
        outs[part][...] = total[64 * (part % 4) : 64 * (part % 4) + 64].astype(BF16)


def feature_kernel(place, act, *refs):
    pieces, (gate_out, up_out), (gg, ug) = refs[:16], refs[16:18], refs[18:]
    assemble(place, pieces, (0, 1), (gg, ug))
    width = gate_out.shape[0]
    contract = (((0,), (0,)), ((), ()))

    @pl.loop(0, gate_out.shape[1] // 256)
    def _(step):
        cols = pl.ds(pl.multiple_of(step * 256, 256), 256)
        tok = act[:, :width]
        gate_out[:, cols] = lax.dot_general(
            tok, gg[:, cols], contract, preferred_element_type=F32
        ).astype(BF16)
        up_out[:, cols] = lax.dot_general(
            tok, ug[:, cols], contract, preferred_element_type=F32
        ).astype(BF16)


def hidden_kernel(place, act, *refs):
    pieces, down_out, hid = refs[:16], refs[16], refs[17]
    assemble(place, pieces, (2,), (hid,))
    width = down_out.shape[1]
    contract = (((0,), (0,)), ((), ()))

    @pl.loop(0, down_out.shape[0] // 256)
    def _(step):
        cols = pl.ds(pl.multiple_of(step * 256, 256), 256)
        down_out[cols, :] = lax.dot_general(
            hid[:, cols], act[:, width:], contract, preferred_element_type=F32
        ).astype(BF16)


def sum_kernel(*refs):
    total = refs[0][...].astype(F32)
    for ref in refs[1:-1]:
        total = total + ref[...].astype(F32)
    refs[-1][...] = total.astype(BF16)


def body(tokens, cotangent, gate, up, down):
    width, hidden = gate.shape
    hid = hidden // 2
    col = lax.axis_index("col")
    place = jnp.stack([lax.rem(col, RING), lax.div(col, RING)]).astype(jnp.int32)
    weights = (gate, up, down)

    mine = jnp.concatenate([tokens, cotangent], axis=1)
    act = jnp.concatenate([mine] + [send_row(mine, -step) for step in range(1, 8)], axis=0)

    piece = ((3, 64, hid), BF16)
    work = 2 * 128 * width * hidden * 3
    far = call(far_kernel, [piece] * 4, (place, act) + weights, flops=work)
    far_got = [send_col(far[2 * h + d], h, 1 - 2 * d) for h in range(2) for d in range(2)]
    near = call(near_kernel, [piece] * 4, (place, act) + weights, flops=work)
    near_got = [send_col(near[2 * h + d], h, 1 - 2 * d) for h in range(2) for d in range(2)]
    relay = call(relay_kernel, [piece] * 4, (place, act) + weights + tuple(far_got), flops=work)
    relay_got = [send_col(relay[2 * h + d], h, 1 - 2 * d) for h in range(2) for d in range(2)]
    got = []
    for h in range(2):
        got += near_got[2 * h : 2 * h + 2] + relay_got[2 * h : 2 * h + 2]
    small = ((3, 32, hid), BF16)
    own = call(
        own_kernel,
        [((3, 32, hid), F32), small, small, small] * 2,
        (place, act) + weights + tuple(got),
        scratch=[pltpu.VMEM((3, 128, hid), F32)],
        flops=work,
    )
    parts = []
    for h in range(2):
        parts.append(own[4 * h])
        parts += [send_col(own[4 * h + step], 1 - h, step) for step in range(1, RING)]
    units = call(unit_kernel, [small] * 2, parts)

    parts = []
    for h in range(2):
        parts.append(units[h])
        parts += [send_col(units[h], 1 - h, step) for step in range(1, RING)]
    joined = call(join_kernel, [piece] * 4, parts)
    pieces = []
    for h in range(2):
        low, high = joined[2 * h : 2 * h + 2]
        low_left, high_right = send_col(low, h, 1), send_col(high, h, -1)
        high_left, low_right = send_col(high, h, 1), send_col(low, h, -1)
        low_far, high_far = send_col(low_left, h, 1), send_col(high_right, h, -1)
        pieces += [low, high, low_left, high_left, low_right, high_right, low_far, high_far]

    tokens_all = act.shape[0]
    whole = pltpu.VMEM((tokens_all, hidden), BF16)
    blocks = call(
        input_kernel,
        [((64, width), BF16)] * 8,
        (place, gate, up) + tuple(pieces),
        scratch=[whole, whole],
        flops=4 * tokens_all * width * hidden,
    )
    input_grad = call(
        sum_kernel,
        [((64, width), BF16)],
        [blocks[0]] + [send_row(blocks[step], step) for step in range(1, 8)],
    )[0]
    gate_term, up_term = call(
        feature_kernel,
        [((width, hidden), BF16)] * 2,
        (place, act) + tuple(pieces),
        scratch=[whole, whole],
        flops=4 * tokens_all * width * hidden,
    )
    down_term = call(
        hidden_kernel,
        [((hidden, width), BF16)],
        (place, act) + tuple(pieces),
        scratch=[whole],
        flops=2 * tokens_all * width * hidden,
    )[0]
    outs = []
    for term in (gate_term, up_term, down_term):
        outs.append((term.astype(F32) + swap_dp(term).astype(F32)).astype(BF16))
    return (input_grad,) + tuple(outs)


def solution(mesh):
    placed = (
        P(("dp", "row"), "col"),
        P(("dp", "row"), "col"),
        P("col", "row"),
        P("col", "row"),
        P("row", "col"),
    )
    return jax.shard_map(
        body,
        mesh=mesh,
        in_specs=placed,
        out_specs=(P(("dp", "row"), "col"), P("col", "row"), P("col", "row"), P("row", "col")),
        check_vma=False,
    )
```

```python
import jax
import jax.numpy as jnp
from jax import lax
from jax.experimental import pallas as pl
from jax.experimental.pallas import tpu as pltpu
from jax.sharding import PartitionSpec as P

RING = 4
BF16 = jnp.bfloat16
F32 = jnp.float32


def send_col(value, axis, step):
    pairs = []
    for dp in range(2):
        for y in range(RING):
            for x in range(RING):
                if axis ^ dp == 0:
                    to = y * RING + (x + step) % RING
                else:
                    to = ((y + step) % RING) * RING + x
                pairs.append((dp * 16 + y * RING + x, dp * 16 + to))
    return lax.ppermute(value, ("dp", "col"), pairs)


def send_row(value, step):
    pairs = []
    for dp in range(2):
        for row in range(8):
            to = (row + step if dp == 0 else row - step) % 8
            pairs.append((dp * 8 + row, dp * 8 + to))
    return lax.ppermute(value, ("dp", "row"), pairs)


def partner(dp, row):
    return (row + 1 if row % 2 == dp else row - 1) % 8


def swap_row(value):
    pairs = [(dp * 8 + row, dp * 8 + partner(dp, row)) for dp in range(2) for row in range(8)]
    return lax.ppermute(value, ("dp", "row"), pairs)


def swap_dp(value):
    return lax.ppermute(value, "dp", [(0, 1), (1, 0)])


def call(kernel, outs, args, scratch=(), flops=0, vmem=24, placed=True):
    whole = pl.BlockSpec(memory_space=pltpu.VMEM)
    small = pl.BlockSpec(memory_space=pltpu.SMEM)
    where = whole if placed else pl.BlockSpec(memory_space=pl.ANY)
    moved = sum(a.size * a.dtype.itemsize for a in args)
    return pl.pallas_call(
        kernel,
        out_shape=[jax.ShapeDtypeStruct(shape, kind) for shape, kind in outs],
        in_specs=[small if a.dtype == jnp.int32 else where for a in args],
        out_specs=[whole] * len(outs),
        scratch_shapes=list(scratch),
        compiler_params=pltpu.CompilerParams(vmem_limit_bytes=vmem * 1024 * 1024),
        cost_estimate=pl.CostEstimate(flops=flops, bytes_accessed=moved, transcendentals=0),
    )(*args)


def rows_of(start, count):
    return pl.ds(pl.multiple_of(start, 32), count)


def pack_kernel(tokens, cotangent, out):
    width = tokens.shape[1]
    out[:, :width] = tokens[...]
    out[:, width:] = cotangent[...]


def bundle_kernel(*refs):
    count = refs[0].shape[0]
    for i in range(4):
        refs[4][count * i : count * i + count] = refs[i][...]


def product_kernel(place, act, gate, up, down, *refs):
    first, outs = refs[:-8], refs[-8:]
    width = gate.shape[0]
    rows = [rows_of(lax.rem(place[0] + step, RING) * 64, 64) for step in (2, 1, 3, 0)]
    both = jnp.concatenate([act[r] for r in rows], axis=0)
    tok, cot = both[:, :width], both[:, width:]
    for k in range(3):
        if k < 2:
            term = jnp.dot(tok, (gate, up)[k][...], preferred_element_type=F32)
        else:
            term = lax.dot_general(
                cot, down[...], (((1,), (1,)), ((), ())), preferred_element_type=F32
            )
        term = term.astype(BF16)
        for q in range(8):
            out = outs[q]
            out[k, out.shape[1] - 32 :] = term[32 * q : 32 * q + 32]
    if first:
        for q in range(8):
            outs[q][:, :32] = first[q][...]


def add_kernel(*refs):
    count = len(refs) // 3
    for i in range(count):
        total = refs[i][...].astype(F32) + refs[count + i][...].astype(F32)
        refs[2 * count + i][...] = total.astype(BF16)


def own_kernel(place, *refs):
    got, outs, held = refs[:6], refs[6:10], refs[10]
    for part in range(2):
        mine, relay, near = got[3 * part : 3 * part + 3]
        total = mine[...].astype(F32) + relay[...].astype(F32) + near[...].astype(F32)
        total = total.astype(BF16)
        held[part] = total[:, :32]
        held[2 + part] = total[:, 32:]
    for step in range(RING):
        outs[step][...] = held[lax.rem(place[1] + step, RING)]


def unit_kernel(own, one, two, three, out):
    gate_sum, up_sum, back_sum = (
        own[k].astype(F32) + one[k].astype(F32) + two[k].astype(F32) + three[k].astype(F32)
        for k in range(3)
    )
    sig = jax.nn.sigmoid(gate_sum)
    silu = gate_sum * sig
    out[0] = (back_sum * up_sum * sig * (1.0 + gate_sum * (1.0 - sig))).astype(BF16)
    out[1] = (back_sum * silu).astype(BF16)
    out[2] = (silu * up_sum).astype(BF16)


def join_kernel(*refs):
    low, high, hid = refs[4:]
    for j in range(4):
        rows = slice(32 * (j % 2), 32 * (j % 2) + 32)
        (low if j < 2 else high)[:, rows] = refs[j][:2]
        hid[32 * j : 32 * j + 32] = refs[j][2]


def rows_at(place, step, j):
    block = lax.rem(place[0] + step, RING)
    sub = lax.rem(place[1] + RING - j, RING)
    return rows_of(256 * lax.div(sub, 2) + 64 * block + 32 * lax.rem(sub, 2), 32)


def assemble(place, pieces, gg, ug):
    for i, step in enumerate((0, 3, 1, 2)):
        for j in range(4):
            piece, lower = pieces[2 * i + j // 2], 32 * (j % 2)
            rows = rows_at(place, step, j)
            gg[rows] = piece[0, lower : lower + 32, :]
            ug[rows] = piece[1, lower : lower + 32, :]


def input_kernel(place, gate, up, *refs):
    pieces, keep, give, gg, ug = refs[:8], *refs[8:]
    assemble(place, pieces, gg, ug)
    contract = (((1,), (1,)), ((), ()))
    total = lax.dot_general(gg[...], gate[...], contract, preferred_element_type=F32)
    total += lax.dot_general(ug[...], up[...], contract, preferred_element_type=F32)
    total = total.astype(BF16)
    rows = keep.shape[0]
    keep[...] = total[:rows]
    give[...] = total[rows:]


def feature_kernel(place, low, high, *refs):
    pieces, gate_out, up_out, act, gg, ug = refs[:8], *refs[8:]
    assemble(place, pieces, gg, ug)
    width, rows = gate_out.shape[0], low.shape[0]
    act[:rows] = low[:, :width]
    act[rows:] = high[:, :width]
    contract = (((0,), (0,)), ((), ()))
    for grad, out in ((gg, gate_out), (ug, up_out)):
        out[...] = lax.dot_general(
            act[...], grad[...], contract, preferred_element_type=F32
        ).astype(BF16)


def hidden_kernel(place, low, high, *refs):
    pieces, down_out, act, hid = refs[:4], *refs[4:]
    for i, step in enumerate((0, 3, 1, 2)):
        for j in range(4):
            hid[rows_at(place, step, j)] = pieces[i][32 * j : 32 * j + 32]
    width, rows = down_out.shape[1], low.shape[0]
    act[:rows] = low[:, width:]
    act[rows:] = high[:, width:]
    contract = (((0,), (0,)), ((), ()))
    down_out[...] = lax.dot_general(
        hid[...], act[...], contract, preferred_element_type=F32
    ).astype(BF16)


def relay_kernel(keep, got, *outs):
    count = outs[0].shape[0]
    for i in range(4):
        rows = slice(count * i, count * i + count)
        outs[i][...] = (keep[rows].astype(F32) + got[rows].astype(F32)).astype(BF16)


def sum_kernel(*refs):
    total = refs[0][...].astype(F32)
    for ref in refs[1:-1]:
        total = total + ref[...].astype(F32)
    refs[-1][...] = total.astype(BF16)


def body(tokens, cotangent, gate, up, down):
    width, hidden = gate.shape
    count = tokens.shape[0]
    rows = 8 * count
    col, row, dp = lax.axis_index("col"), lax.axis_index("row"), lax.axis_index("dp")
    x, y = lax.rem(col, RING), lax.div(col, RING)
    here, other = jnp.where(dp == 0, x, y), jnp.where(dp == 0, y, x)
    place = jnp.stack([here, other]).astype(jnp.int32)

    mine = call(pack_kernel, [((count, 2 * width), BF16)], (tokens, cotangent))[0]
    evens = [mine] + [send_row(mine, -2 * i) for i in range(1, 4)]
    even = call(bundle_kernel, [((4 * count, 2 * width), BF16)], evens)[0]
    odd = swap_row(even)

    third, half = ((3, 32, hidden), BF16), ((3, 64, hidden), BF16)
    part = ()
    for act, kind in ((even, third), (odd, half)):
        part = call(
            product_kernel,
            [kind] * 8,
            (place, act, gate, up, down) + tuple(part),
            flops=2 * 256 * width * hidden * 3,
        )
    far_up, far_down, pass_up, near_up, near_down, pass_down, low, high = part
    far_up, far_down = send_col(far_up, 0, 1), send_col(far_down, 0, -1)
    near_up, near_down = send_col(near_up, 0, 1), send_col(near_down, 0, -1)
    relay = call(add_kernel, [half] * 2, (pass_up, pass_down, far_up, far_down))
    relay_up, relay_down = send_col(relay[0], 0, 1), send_col(relay[1], 0, -1)
    own = call(
        own_kernel,
        [third] * 4,
        (place, low, relay_up, near_down, high, relay_down, near_up),
        scratch=[pltpu.VMEM((4, 3, 32, hidden), BF16)],
    )
    got = [own[0]] + [send_col(own[step], 1, step) for step in range(1, RING)]
    unit = call(unit_kernel, [third], got)[0]
    got = [unit] + [send_col(unit, 1, step) for step in range(1, RING)]
    low, high, hid = call(
        join_kernel,
        [((2, 64, hidden), BF16)] * 2 + [((128, hidden), BF16)],
        got,
    )
    low_left, high_right = send_col(low, 0, 1), send_col(high, 0, -1)
    low, high, low_left, high_right = lax.optimization_barrier((low, high, low_left, high_right))
    low_far, high_far = send_col(low_left, 0, 1), send_col(high_right, 0, -1)
    high_left, low_right = send_col(high, 0, 1), send_col(low, 0, -1)
    hid, high_left, low_right = lax.optimization_barrier((hid, high_left, low_right))
    pieces = (low, high, low_left, high_left, low_right, high_right, low_far, high_far)
    hids = (hid, send_col(hid, 0, 1), send_col(hid, 0, -1), send_col(hid, 0, 2))

    whole = pltpu.VMEM((rows, hidden), BF16)
    lhs = pltpu.VMEM((rows, width), BF16)
    work = 2 * rows * width * hidden
    keep, give = call(
        input_kernel,
        [((4 * count, width), BF16)] * 2,
        (place, gate, up) + pieces,
        scratch=[whole, whole],
        flops=2 * work,
    )
    keep, give, pieces = lax.optimization_barrier((keep, give, pieces))
    swapped = swap_row(give)
    features = call(
        feature_kernel,
        [((width, hidden), BF16)] * 2,
        (place, even, odd) + pieces,
        scratch=[lhs, whole, whole],
        flops=2 * work,
    )
    swapped, *features = lax.optimization_barrier((swapped, *features))
    block = ((count, width), BF16)
    sums = call(relay_kernel, [block] * 4, (keep, swapped))
    sums, hids = lax.optimization_barrier((sums, hids))
    outs = [
        call(sum_kernel, [(term.shape, BF16)], (term, swap_dp(term)))[0] for term in features
    ]
    down_term = call(
        hidden_kernel,
        [((hidden, width), BF16)],
        (place, even, odd) + hids,
        scratch=[lhs, whole],
        flops=work,
    )[0]
    got = [sums[0]] + [send_row(sums[i], 2 * i) for i in range(1, 3)]
    last, *outs = lax.optimization_barrier((sums[3], *outs))
    got.append(send_row(last, 6))
    input_grad = call(sum_kernel, [block], got)[0]
    outs.append(
        call(sum_kernel, [(down_term.shape, BF16)], (down_term, swap_dp(down_term)))[0]
    )
    return (input_grad,) + tuple(outs)


def solution(mesh):
    placed = (
        P(("dp", "row"), "col"),
        P(("dp", "row"), "col"),
        P("col", "row"),
        P("col", "row"),
        P("row", "col"),
    )
    return jax.shard_map(
        body,
        mesh=mesh,
        in_specs=placed,
        out_specs=(P(("dp", "row"), "col"), P("col", "row"), P("col", "row"), P("row", "col")),
        check_vma=False,
    )
```

```python
import functools

import jax
import jax.numpy as jnp
from jax import lax
from jax.experimental import pallas as pl
from jax.experimental.pallas import tpu as pltpu
from jax.sharding import PartitionSpec as P

RING = 4
MERGE = 8
BF16 = jnp.bfloat16
F32 = jnp.float32


def send_col(value, axis, step):
    pairs = []
    for dp in range(2):
        for y in range(RING):
            for x in range(RING):
                if axis ^ dp == 0:
                    to = y * RING + (x + step) % RING
                else:
                    to = ((y + step) % RING) * RING + x
                pairs.append((dp * 16 + y * RING + x, dp * 16 + to))
    return lax.ppermute(value, ("dp", "col"), pairs)


def send_row(value, step):
    pairs = []
    for dp in range(2):
        for row in range(8):
            to = (row + step if dp == 0 else row - step) % 8
            pairs.append((dp * 8 + row, dp * 8 + to))
    return lax.ppermute(value, ("dp", "row"), pairs)


def partner(dp, row):
    return (row + 1 if row % 2 == dp else row - 1) % 8


def swap_row(value):
    pairs = [(dp * 8 + row, dp * 8 + partner(dp, row)) for dp in range(2) for row in range(8)]
    return lax.ppermute(value, ("dp", "row"), pairs)


def swap_dp(value):
    return lax.ppermute(value, "dp", [(0, 1), (1, 0)])


def call(kernel, outs, args, scratch=(), flops=0, vmem=24, placed=True):
    whole = pl.BlockSpec(memory_space=pltpu.VMEM)
    small = pl.BlockSpec(memory_space=pltpu.SMEM)
    where = whole if placed else pl.BlockSpec(memory_space=pl.ANY)
    moved = sum(a.size * a.dtype.itemsize for a in args)
    return pl.pallas_call(
        kernel,
        out_shape=[jax.ShapeDtypeStruct(shape, kind) for shape, kind in outs],
        in_specs=[small if a.dtype == jnp.int32 else where for a in args],
        out_specs=[whole] * len(outs),
        scratch_shapes=list(scratch),
        compiler_params=pltpu.CompilerParams(vmem_limit_bytes=vmem * 1024 * 1024),
        cost_estimate=pl.CostEstimate(flops=flops, bytes_accessed=moved, transcendentals=0),
    )(*args)


def rows_of(start, count):
    return pl.ds(pl.multiple_of(start, 32), count)


def pack_kernel(tokens, cotangent, out):
    width = tokens.shape[1]
    out[:, :width] = tokens[...]
    out[:, width:] = cotangent[...]


def bundle_kernel(*refs):
    count = refs[0].shape[0]
    for i in range(4):
        refs[4][count * i : count * i + count] = refs[i][...]


def product_kernel(steps, place, act, gate, up, down, *refs):
    groups = 2 * len(steps)
    first, outs = refs[:-groups], refs[-groups:]
    width = gate.shape[0]
    rows = [rows_of(lax.rem(place[0] + step, RING) * 64, 64) for step in steps]
    both = jnp.concatenate([act[r] for r in rows], axis=0)
    tok, cot = both[:, :width], both[:, width:]
    for k in range(3):
        if k < 2:
            term = jnp.dot(tok, (gate, up)[k][...], preferred_element_type=F32)
        else:
            term = lax.dot_general(
                cot, down[...], (((1,), (1,)), ((), ())), preferred_element_type=F32
            )
        term = term.astype(BF16)
        for q in range(groups):
            out = outs[q]
            out[k, out.shape[1] - 32 :] = term[32 * q : 32 * q + 32]
    if first:
        for q in range(groups):
            outs[q][:, :32] = first[q][...]


def add_kernel(*refs):
    count = len(refs) // 3
    for i in range(count):
        total = refs[i][...].astype(F32) + refs[count + i][...].astype(F32)
        refs[2 * count + i][...] = total.astype(BF16)


def own_kernel(place, *refs):
    got, outs, held = refs[:6], refs[6:10], refs[10]
    for part in range(2):
        mine, relay, near = got[3 * part : 3 * part + 3]
        total = mine[...].astype(F32) + relay[...].astype(F32) + near[...].astype(F32)
        total = total.astype(BF16)
        held[part] = total[:, :32]
        held[2 + part] = total[:, 32:]
    for step in range(RING):
        outs[step][...] = held[lax.rem(place[1] + step, RING)]


def unit_kernel(own, one, two, three, out):
    gate_sum, up_sum, back_sum = (
        own[k].astype(F32) + one[k].astype(F32) + two[k].astype(F32) + three[k].astype(F32)
        for k in range(3)
    )
    sig = jax.nn.sigmoid(gate_sum)
    silu = gate_sum * sig
    out[0] = (back_sum * up_sum * sig * (1.0 + gate_sum * (1.0 - sig))).astype(BF16)
    out[1] = (back_sum * silu).astype(BF16)
    out[2] = (silu * up_sum).astype(BF16)


def join_kernel(*refs):
    low, high, hid = refs[4:]
    for j in range(4):
        rows = slice(32 * (j % 2), 32 * (j % 2) + 32)
        (low if j < 2 else high)[:, rows] = refs[j][:2]
        hid[32 * j : 32 * j + 32] = refs[j][2]


def rows_at(place, step, j):
    block = lax.rem(place[0] + step, RING)
    sub = lax.rem(place[1] + RING - j, RING)
    return rows_of(256 * lax.div(sub, 2) + 64 * block + 32 * lax.rem(sub, 2), 32)


def assemble(place, pieces, gg, ug):
    for i, step in enumerate((0, 3, 1, 2)):
        for j in range(4):
            piece, lower = pieces[2 * i + j // 2], 32 * (j % 2)
            rows = rows_at(place, step, j)
            gg[rows] = piece[0, lower : lower + 32, :]
            ug[rows] = piece[1, lower : lower + 32, :]


def give_kernel(place, gate, up, *refs):
    pieces, out, gg, ug = refs[:8], *refs[8:]
    assemble(place, pieces, gg, ug)
    out[...] = input_sum(gg[out.shape[0] :], ug[out.shape[0] :], gate, up).astype(BF16)


def input_sum(gg, ug, gate, up):
    contract = (((1,), (1,)), ((), ()))
    total = lax.dot_general(gg, gate[...], contract, preferred_element_type=F32)
    return total + lax.dot_general(ug, up[...], contract, preferred_element_type=F32)


def keep_kernel(gate, up, gg, ug, out):
    rows = out.shape[0]
    out[...] = input_sum(gg[:rows], ug[:rows], gate, up)


def feature_kernel(low, high, gg, ug, gate_out, up_out, act):
    width, rows = gate_out.shape[0], low.shape[0]
    act[:rows] = low[:, :width]
    act[rows:] = high[:, :width]
    contract = (((0,), (0,)), ((), ()))
    for grad, out in ((gg, gate_out), (ug, up_out)):
        out[...] = lax.dot_general(
            act[...], grad[...], contract, preferred_element_type=F32
        ).astype(BF16)


def hidden_kernel(place, low, high, *refs):
    pieces, down_out, act, hid = refs[:4], *refs[4:]
    for i, step in enumerate((0, 3, 1, 2)):
        for j in range(4):
            hid[rows_at(place, step, j)] = pieces[i][32 * j : 32 * j + 32]
    width, rows = down_out.shape[1], low.shape[0]
    act[:rows] = low[:, width:]
    act[rows:] = high[:, width:]
    contract = (((0,), (0,)), ((), ()))
    down_out[...] = lax.dot_general(
        hid[...], act[...], contract, preferred_element_type=F32
    ).astype(BF16)


def split_kernel(keep, got, *outs):
    count = outs[0].shape[0]
    for i in range(4):
        rows = slice(count * i, count * i + count)
        outs[i][...] = (keep[rows] + got[rows].astype(F32)).astype(BF16)


def sum_kernel(*refs):
    total = refs[0][...].astype(F32)
    for ref in refs[1:-1]:
        total = total + ref[...].astype(F32)
    refs[-1][...] = total.astype(BF16)


def merge_kernel(mine, got, out, held, sems):
    count = mine.shape[0] // MERGE
    copies = []
    for i in range(MERGE):
        rows = pl.ds(count * i, count)
        held[rows] = (mine[rows].astype(F32) + got[rows].astype(F32)).astype(BF16)
        copies.append(pltpu.make_async_copy(held.at[rows], out.at[rows], sems.at[i]))
        copies[-1].start()
    for copy in copies:
        copy.wait()


def merge(term):
    return pl.pallas_call(
        merge_kernel,
        out_shape=jax.ShapeDtypeStruct(term.shape, BF16),
        in_specs=[pl.BlockSpec(memory_space=pltpu.VMEM)] * 2,
        out_specs=pl.BlockSpec(memory_space=pl.ANY),
        scratch_shapes=[pltpu.VMEM(term.shape, BF16), pltpu.SemaphoreType.DMA((MERGE,))],
        compiler_params=pltpu.CompilerParams(vmem_limit_bytes=24 * 1024 * 1024),
    )(term, swap_dp(term))


def body(tokens, cotangent, gate, up, down):
    width, hidden = gate.shape
    count = tokens.shape[0]
    rows = 8 * count
    col, row, dp = lax.axis_index("col"), lax.axis_index("row"), lax.axis_index("dp")
    x, y = lax.rem(col, RING), lax.div(col, RING)
    here, other = jnp.where(dp == 0, x, y), jnp.where(dp == 0, y, x)
    place = jnp.stack([here, other]).astype(jnp.int32)

    mine = call(pack_kernel, [((count, 2 * width), BF16)], (tokens, cotangent))[0]
    evens = [mine] + [send_row(mine, -2 * i) for i in range(1, 4)]
    even = call(bundle_kernel, [((4 * count, 2 * width), BF16)], evens)[0]
    odd = swap_row(even)

    third, half = ((3, 32, hidden), BF16), ((3, 64, hidden), BF16)
    weights = (gate, up, down)

    def products(steps, kind, act, earlier):
        return call(
            functools.partial(product_kernel, steps),
            [kind] * (2 * len(steps)),
            (place, act) + weights + tuple(earlier),
            flops=2 * 64 * len(steps) * width * hidden * 3,
        )

    part = products((2, 1, 3, 0), third, even, ())
    part = products((2,), half, odd, part[:2]) + products((1, 3, 0), half, odd, part[2:])
    far_up, far_down, pass_up, near_up, near_down, pass_down, low, high = part
    far_up, far_down = send_col(far_up, 0, 1), send_col(far_down, 0, -1)
    near_up, near_down = send_col(near_up, 0, 1), send_col(near_down, 0, -1)
    relay = call(add_kernel, [half] * 2, (pass_up, pass_down, far_up, far_down))
    relay_up, relay_down = send_col(relay[0], 0, 1), send_col(relay[1], 0, -1)
    own = call(
        own_kernel,
        [third] * 4,
        (place, low, relay_up, near_down, high, relay_down, near_up),
        scratch=[pltpu.VMEM((4, 3, 32, hidden), BF16)],
    )
    got = [own[0]] + [send_col(own[step], 1, step) for step in range(1, RING)]
    unit = call(unit_kernel, [third], got)[0]
    got = [unit] + [send_col(unit, 1, step) for step in range(1, RING)]
    low, high, hid = call(
        join_kernel,
        [((2, 64, hidden), BF16)] * 2 + [((128, hidden), BF16)],
        got,
    )
    low_left, high_right = send_col(low, 0, 1), send_col(high, 0, -1)
    low, high, low_left, high_right = lax.optimization_barrier((low, high, low_left, high_right))
    low_far, high_far = send_col(low_left, 0, 1), send_col(high_right, 0, -1)
    high_left, low_right = send_col(high, 0, 1), send_col(low, 0, -1)
    hid, high_left, low_right = lax.optimization_barrier((hid, high_left, low_right))
    pieces = (low, high, low_left, high_left, low_right, high_right, low_far, high_far)
    hids = (hid, send_col(hid, 0, 1), send_col(hid, 0, -1), send_col(hid, 0, 2))

    whole = pltpu.VMEM((rows, hidden), BF16)
    lhs = pltpu.VMEM((rows, width), BF16)
    work = 2 * rows * width * hidden
    give, gg, ug = call(
        give_kernel,
        [((4 * count, width), BF16)] + [((rows, hidden), BF16)] * 2,
        (place, gate, up) + pieces,
        flops=work,
    )
    swapped = swap_row(give)
    keep = call(keep_kernel, [((4 * count, width), F32)], (gate, up, gg, ug), flops=work)[0]
    features = call(
        feature_kernel,
        [((width, hidden), BF16)] * 2,
        (even, odd, gg, ug),
        scratch=[lhs],
        flops=2 * work,
    )
    swapped, keep, *features = lax.optimization_barrier((swapped, keep, *features))
    block = ((count, width), BF16)
    sums = call(split_kernel, [block] * 4, (keep, swapped))
    sums, hids = lax.optimization_barrier((sums, hids))
    outs = [merge(term) for term in features]
    down_term = call(
        hidden_kernel,
        [((hidden, width), BF16)],
        (place, even, odd) + hids,
        scratch=[lhs, whole],
        flops=work,
    )[0]
    got = [sums[0]] + [send_row(sums[i], 2 * i) for i in range(1, 4)]
    got, outs = lax.optimization_barrier((got, outs))
    input_grad = call(sum_kernel, [block], got)[0]
    outs = list(outs) + [merge(down_term)]
    return (input_grad,) + tuple(outs)


def solution(mesh):
    placed = (
        P(("dp", "row"), "col"),
        P(("dp", "row"), "col"),
        P("col", "row"),
        P("col", "row"),
        P("row", "col"),
    )
    return jax.shard_map(
        body,
        mesh=mesh,
        in_specs=placed,
        out_specs=(P(("dp", "row"), "col"), P("col", "row"), P("col", "row"), P("row", "col")),
        check_vma=False,
    )
```

```python
import functools

import jax
import jax.numpy as jnp
from jax import lax
from jax.experimental import pallas as pl
from jax.experimental.pallas import tpu as pltpu
from jax.sharding import PartitionSpec as P

RING = 4
MERGE = 8
BF16 = jnp.bfloat16
F32 = jnp.float32


def send_col(value, axis, step):
    pairs = []
    for dp in range(2):
        for y in range(RING):
            for x in range(RING):
                if axis ^ dp == 0:
                    to = y * RING + (x + step) % RING
                else:
                    to = ((y + step) % RING) * RING + x
                pairs.append((dp * 16 + y * RING + x, dp * 16 + to))
    return lax.ppermute(value, ("dp", "col"), pairs)


def send_row(value, step):
    pairs = []
    for dp in range(2):
        for row in range(8):
            to = (row + step if dp == 0 else row - step) % 8
            pairs.append((dp * 8 + row, dp * 8 + to))
    return lax.ppermute(value, ("dp", "row"), pairs)


def partner(dp, row):
    return (row + 1 if row % 2 == dp else row - 1) % 8


def swap_row(value):
    pairs = [(dp * 8 + row, dp * 8 + partner(dp, row)) for dp in range(2) for row in range(8)]
    return lax.ppermute(value, ("dp", "row"), pairs)


def swap_dp(value):
    return lax.ppermute(value, "dp", [(0, 1), (1, 0)])


def call(kernel, outs, args, scratch=(), flops=0, vmem=24, placed=True):
    whole = pl.BlockSpec(memory_space=pltpu.VMEM)
    small = pl.BlockSpec(memory_space=pltpu.SMEM)
    where = whole if placed else pl.BlockSpec(memory_space=pl.ANY)
    moved = sum(a.size * a.dtype.itemsize for a in args)
    return pl.pallas_call(
        kernel,
        out_shape=[jax.ShapeDtypeStruct(shape, kind) for shape, kind in outs],
        in_specs=[small if a.dtype == jnp.int32 else where for a in args],
        out_specs=[whole] * len(outs),
        scratch_shapes=list(scratch),
        compiler_params=pltpu.CompilerParams(vmem_limit_bytes=vmem * 1024 * 1024),
        cost_estimate=pl.CostEstimate(flops=flops, bytes_accessed=moved, transcendentals=0),
    )(*args)


def rows_of(start, count):
    return pl.ds(pl.multiple_of(start, 32), count)


def pack_kernel(tokens, cotangent, out):
    width = tokens.shape[1]
    out[:, :width] = tokens[...]
    out[:, width:] = cotangent[...]


def bundle_kernel(*refs):
    count = refs[0].shape[0]
    for i in range(4):
        refs[4][count * i : count * i + count] = refs[i][...]


def product_kernel(steps, place, act, gate, up, down, *refs):
    groups = 2 * len(steps)
    first, outs = refs[:-groups], refs[-groups:]
    width = gate.shape[0]
    rows = [rows_of(lax.rem(place[0] + step, RING) * 64, 64) for step in steps]
    both = jnp.concatenate([act[r] for r in rows], axis=0)
    tok, cot = both[:, :width], both[:, width:]
    for k in range(3):
        if k < 2:
            term = jnp.dot(tok, (gate, up)[k][...], preferred_element_type=F32)
        else:
            term = lax.dot_general(
                cot, down[...], (((1,), (1,)), ((), ())), preferred_element_type=F32
            )
        term = term.astype(BF16)
        for q in range(groups):
            out = outs[q]
            out[k, out.shape[1] - 32 :] = term[32 * q : 32 * q + 32]
    if first:
        for q in range(groups):
            outs[q][:, :32] = first[q][...]


def add_kernel(*refs):
    count = len(refs) // 3
    for i in range(count):
        total = refs[i][...].astype(F32) + refs[count + i][...].astype(F32)
        refs[2 * count + i][...] = total.astype(BF16)


def own_kernel(place, *refs):
    got, outs, held = refs[:6], refs[6:10], refs[10]
    for part in range(2):
        mine, relay, near = got[3 * part : 3 * part + 3]
        total = mine[...].astype(F32) + relay[...].astype(F32) + near[...].astype(F32)
        total = total.astype(BF16)
        held[part] = total[:, :32]
        held[2 + part] = total[:, 32:]
    for step in range(RING):
        outs[step][...] = held[lax.rem(place[1] + step, RING)]


def unit_kernel(own, one, two, three, out):
    gate_sum, up_sum, back_sum = (
        own[k].astype(F32) + one[k].astype(F32) + two[k].astype(F32) + three[k].astype(F32)
        for k in range(3)
    )
    sig = jax.nn.sigmoid(gate_sum)
    silu = gate_sum * sig
    out[0] = (back_sum * up_sum * sig * (1.0 + gate_sum * (1.0 - sig))).astype(BF16)
    out[1] = (back_sum * silu).astype(BF16)
    out[2] = (silu * up_sum).astype(BF16)


def join_kernel(*refs):
    low, high, hid = refs[4:]
    for j in range(4):
        rows = slice(32 * (j % 2), 32 * (j % 2) + 32)
        (low if j < 2 else high)[:, rows] = refs[j][:2]
        hid[32 * j : 32 * j + 32] = refs[j][2]


def rows_at(place, step, j):
    block = lax.rem(place[0] + step, RING)
    sub = lax.rem(place[1] + RING - j, RING)
    return rows_of(256 * lax.div(sub, 2) + 64 * block + 32 * lax.rem(sub, 2), 32)


def assemble(place, pieces, gg, ug):
    for i, step in enumerate((0, 3, 1, 2)):
        for j in range(4):
            piece, lower = pieces[2 * i + j // 2], 32 * (j % 2)
            rows = rows_at(place, step, j)
            gg[rows] = piece[0, lower : lower + 32, :]
            ug[rows] = piece[1, lower : lower + 32, :]


def give_kernel(place, gate, up, *refs):
    pieces, out, gg, ug = refs[:8], *refs[8:]
    assemble(place, pieces, gg, ug)
    out[...] = input_sum(gg[out.shape[0] :], ug[out.shape[0] :], gate, up).astype(BF16)


def input_sum(gg, ug, gate, up):
    contract = (((1,), (1,)), ((), ()))
    total = lax.dot_general(gg, gate[...], contract, preferred_element_type=F32)
    return total + lax.dot_general(ug, up[...], contract, preferred_element_type=F32)


def keep_kernel(gate, up, gg, ug, out):
    rows = out.shape[0]
    out[...] = input_sum(gg[:rows], ug[:rows], gate, up)


def feature_kernel(low, high, gg, ug, gate_out, up_out, act):
    width, rows = gate_out.shape[0], low.shape[0]
    act[:rows] = low[:, :width]
    act[rows:] = high[:, :width]
    contract = (((0,), (0,)), ((), ()))
    for grad, out in ((gg, gate_out), (ug, up_out)):
        out[...] = lax.dot_general(
            act[...], grad[...], contract, preferred_element_type=F32
        ).astype(BF16)


def hidden_kernel(place, low, high, *refs):
    pieces, down_out, act, hid = refs[:4], *refs[4:]
    for i, step in enumerate((0, 3, 1, 2)):
        for j in range(4):
            hid[rows_at(place, step, j)] = pieces[i][32 * j : 32 * j + 32]
    width, rows = down_out.shape[1], low.shape[0]
    act[:rows] = low[:, width:]
    act[rows:] = high[:, width:]
    contract = (((0,), (0,)), ((), ()))
    down_out[...] = lax.dot_general(
        hid[...], act[...], contract, preferred_element_type=F32
    ).astype(BF16)


def split_kernel(keep, got, *outs):
    count = outs[0].shape[0]
    for i in range(4):
        rows = slice(count * i, count * i + count)
        outs[i][...] = (keep[rows] + got[rows].astype(F32)).astype(BF16)


def sum_kernel(*refs):
    total = refs[0][...].astype(F32)
    for ref in refs[1:-1]:
        total = total + ref[...].astype(F32)
    refs[-1][...] = total.astype(BF16)


def merge_kernel(mine, got, out, held, sems):
    count = mine.shape[0] // MERGE
    copies = []
    for i in range(MERGE):
        rows = pl.ds(count * i, count)
        held[rows] = (mine[rows].astype(F32) + got[rows].astype(F32)).astype(BF16)
        copies.append(pltpu.make_async_copy(held.at[rows], out.at[rows], sems.at[i]))
        copies[-1].start()
    for copy in copies:
        copy.wait()


def merge(term):
    return pl.pallas_call(
        merge_kernel,
        out_shape=jax.ShapeDtypeStruct(term.shape, BF16),
        in_specs=[pl.BlockSpec(memory_space=pltpu.VMEM)] * 2,
        out_specs=pl.BlockSpec(memory_space=pl.ANY),
        scratch_shapes=[pltpu.VMEM(term.shape, BF16), pltpu.SemaphoreType.DMA((MERGE,))],
        compiler_params=pltpu.CompilerParams(vmem_limit_bytes=24 * 1024 * 1024),
    )(term, swap_dp(term))


def body(tokens, cotangent, gate, up, down):
    width, hidden = gate.shape
    count = tokens.shape[0]
    rows = 8 * count
    col, row, dp = lax.axis_index("col"), lax.axis_index("row"), lax.axis_index("dp")
    x, y = lax.rem(col, RING), lax.div(col, RING)
    here, other = jnp.where(dp == 0, x, y), jnp.where(dp == 0, y, x)
    place = jnp.stack([here, other]).astype(jnp.int32)

    mine = call(pack_kernel, [((count, 2 * width), BF16)], (tokens, cotangent))[0]
    evens = [mine] + [send_row(mine, -2 * i) for i in range(1, 4)]
    even = call(bundle_kernel, [((4 * count, 2 * width), BF16)], evens)[0]
    odd = swap_row(even)

    third, half = ((3, 32, hidden), BF16), ((3, 64, hidden), BF16)
    weights = (gate, up, down)

    def products(steps, kind, act, earlier):
        return call(
            functools.partial(product_kernel, steps),
            [kind] * (2 * len(steps)),
            (place, act) + weights + tuple(earlier),
            flops=2 * 64 * len(steps) * width * hidden * 3,
        )

    part = products((2, 1, 3, 0), third, even, ())
    part = products((2,), half, odd, part[:2]) + products((1, 3, 0), half, odd, part[2:])
    far_up, far_down, pass_up, near_up, near_down, pass_down, low, high = part
    far_up, far_down = send_col(far_up, 0, 1), send_col(far_down, 0, -1)
    near_up, near_down = send_col(near_up, 0, 1), send_col(near_down, 0, -1)
    relay = call(add_kernel, [half] * 2, (pass_up, pass_down, far_up, far_down))
    relay_up, relay_down = send_col(relay[0], 0, 1), send_col(relay[1], 0, -1)
    own = call(
        own_kernel,
        [third] * 4,
        (place, low, relay_up, near_down, high, relay_down, near_up),
        scratch=[pltpu.VMEM((4, 3, 32, hidden), BF16)],
    )
    got = [own[0]] + [send_col(own[step], 1, step) for step in range(1, RING)]
    unit = call(unit_kernel, [third], got)[0]
    got = [unit] + [send_col(unit, 1, step) for step in range(1, RING)]
    low, high, hid = call(
        join_kernel,
        [((2, 64, hidden), BF16)] * 2 + [((128, hidden), BF16)],
        got,
    )
    low_left, high_right = send_col(low, 0, 1), send_col(high, 0, -1)
    high_left, low_right = send_col(high, 0, 1), send_col(low, 0, -1)
    low_far, high_far = send_col(low_left, 0, 1), send_col(high_right, 0, -1)
    hid, high_left, low_right = lax.optimization_barrier((hid, high_left, low_right))
    pieces = (low, high, low_left, high_left, low_right, high_right, low_far, high_far)
    hids = (hid, send_col(hid, 0, 1), send_col(hid, 0, -1), send_col(hid, 0, 2))

    whole = pltpu.VMEM((rows, hidden), BF16)
    lhs = pltpu.VMEM((rows, width), BF16)
    work = 2 * rows * width * hidden
    give, gg, ug = call(
        give_kernel,
        [((4 * count, width), BF16)] + [((rows, hidden), BF16)] * 2,
        (place, gate, up) + pieces,
        flops=work,
    )
    swapped = swap_row(give)
    keep = call(keep_kernel, [((4 * count, width), F32)], (gate, up, gg, ug), flops=work)[0]
    features = call(
        feature_kernel,
        [((width, hidden), BF16)] * 2,
        (even, odd, gg, ug),
        scratch=[lhs],
        flops=2 * work,
    )
    swapped, keep, *features = lax.optimization_barrier((swapped, keep, *features))
    block = ((count, width), BF16)
    sums = call(split_kernel, [block] * 4, (keep, swapped))
    sums, hids = lax.optimization_barrier((sums, hids))
    outs = [merge(term) for term in features]
    down_term = call(
        hidden_kernel,
        [((hidden, width), BF16)],
        (place, even, odd) + hids,
        scratch=[lhs, whole],
        flops=work,
    )[0]
    got = [sums[0]] + [send_row(sums[i], 2 * i) for i in range(1, 4)]
    got, outs = lax.optimization_barrier((got, outs))
    input_grad = call(sum_kernel, [block], got)[0]
    outs = list(outs) + [merge(down_term)]
    return (input_grad,) + tuple(outs)


def solution(mesh):
    placed = (
        P(("dp", "row"), "col"),
        P(("dp", "row"), "col"),
        P("col", "row"),
        P("col", "row"),
        P("row", "col"),
    )
    return jax.shard_map(
        body,
        mesh=mesh,
        in_specs=placed,
        out_specs=(P(("dp", "row"), "col"), P("col", "row"), P("col", "row"), P("row", "col")),
        check_vma=False,
    )
```

```python
import functools

import jax
import jax.numpy as jnp
from jax import lax
from jax.experimental import pallas as pl
from jax.experimental.pallas import tpu as pltpu
from jax.sharding import PartitionSpec as P

RING = 4
STEPS = (2, 1, 3)
MERGE = 8
BF16 = jnp.bfloat16
F32 = jnp.float32


def send_col(value, axis, step):
    pairs = []
    for dp in range(2):
        for y in range(RING):
            for x in range(RING):
                if axis ^ dp == 0:
                    to = y * RING + (x + step) % RING
                else:
                    to = ((y + step) % RING) * RING + x
                pairs.append((dp * 16 + y * RING + x, dp * 16 + to))
    return lax.ppermute(value, ("dp", "col"), pairs)


def send_row(value, step):
    pairs = []
    for dp in range(2):
        for row in range(8):
            to = (row + step if dp == 0 else row - step) % 8
            pairs.append((dp * 8 + row, dp * 8 + to))
    return lax.ppermute(value, ("dp", "row"), pairs)


def partner(dp, row):
    return (row + 1 if row % 2 == dp else row - 1) % 8


def swap_row(value):
    pairs = [(dp * 8 + row, dp * 8 + partner(dp, row)) for dp in range(2) for row in range(8)]
    return lax.ppermute(value, ("dp", "row"), pairs)


def swap_dp(value):
    return lax.ppermute(value, "dp", [(0, 1), (1, 0)])


def call(kernel, outs, args, scratch=(), flops=0, vmem=24, placed=True):
    whole = pl.BlockSpec(memory_space=pltpu.VMEM)
    small = pl.BlockSpec(memory_space=pltpu.SMEM)
    where = whole if placed else pl.BlockSpec(memory_space=pl.ANY)
    moved = sum(a.size * a.dtype.itemsize for a in args)
    return pl.pallas_call(
        kernel,
        out_shape=[jax.ShapeDtypeStruct(shape, kind) for shape, kind in outs],
        in_specs=[small if a.dtype == jnp.int32 else where for a in args],
        out_specs=[whole] * len(outs),
        scratch_shapes=list(scratch),
        compiler_params=pltpu.CompilerParams(vmem_limit_bytes=vmem * 1024 * 1024),
        cost_estimate=pl.CostEstimate(flops=flops, bytes_accessed=moved, transcendentals=0),
    )(*args)


def rows_of(start, count):
    return pl.ds(pl.multiple_of(start, 32), count)


def pack_kernel(tokens, cotangent, out):
    width = tokens.shape[1]
    out[:, :width] = tokens[...]
    out[:, width:] = cotangent[...]


def bundle_kernel(*refs):
    count = refs[0].shape[0]
    for i in range(4):
        refs[4][count * i : count * i + count] = refs[i][...]


def product_kernel(steps, place, act, gate, up, down, *refs):
    groups = 2 * len(steps)
    first, outs = refs[:-groups], refs[-groups:]
    width = gate.shape[0]
    rows = [rows_of(lax.rem(place[0] + step, RING) * 64, 64) for step in steps]
    both = jnp.concatenate([act[r] for r in rows], axis=0)
    tok, cot = both[:, :width], both[:, width:]
    for k in range(3):
        if k < 2:
            term = jnp.dot(tok, (gate, up)[k][...], preferred_element_type=F32)
        else:
            term = lax.dot_general(
                cot, down[...], (((1,), (1,)), ((), ())), preferred_element_type=F32
            )
        term = term.astype(BF16)
        for q in range(groups):
            out = outs[q]
            out[k, out.shape[1] - 32 :] = term[32 * q : 32 * q + 32]
    if first:
        for q in range(groups):
            outs[q][:, :32] = first[q][...]


def add_kernel(*refs):
    count = len(refs) // 3
    for i in range(count):
        total = refs[i][...].astype(F32) + refs[count + i][...].astype(F32)
        refs[2 * count + i][...] = total.astype(BF16)


def own_kernel(place, *refs):
    got, outs, held = refs[:6], refs[6:10], refs[10]
    for part in range(2):
        mine, relay, near = got[3 * part : 3 * part + 3]
        total = mine[...].astype(F32) + relay[...].astype(F32) + near[...].astype(F32)
        total = total.astype(BF16)
        held[part] = total[:, :32]
        held[2 + part] = total[:, 32:]
    for step in range(RING):
        outs[step][...] = held[lax.rem(place[1] + step, RING)]


def unit_kernel(own, one, two, three, out):
    gate_sum, up_sum, back_sum = (
        own[k].astype(F32) + one[k].astype(F32) + two[k].astype(F32) + three[k].astype(F32)
        for k in range(3)
    )
    sig = jax.nn.sigmoid(gate_sum)
    silu = gate_sum * sig
    out[0] = (back_sum * up_sum * sig * (1.0 + gate_sum * (1.0 - sig))).astype(BF16)
    out[1] = (back_sum * silu).astype(BF16)
    out[2] = (silu * up_sum).astype(BF16)


def join_kernel(*refs):
    low, high, hid = refs[4:]
    for j, ref in zip((0,) + STEPS, refs):
        rows = slice(32 * (j % 2), 32 * (j % 2) + 32)
        (low if j < 2 else high)[:, rows] = ref[:2]
        hid[32 * j : 32 * j + 32] = ref[2]


def rows_at(place, step, j):
    block = lax.rem(place[0] + step, RING)
    sub = lax.rem(place[1] + RING - j, RING)
    return rows_of(256 * lax.div(sub, 2) + 64 * block + 32 * lax.rem(sub, 2), 32)


def assemble(place, pieces, gg, ug):
    for i, step in enumerate((0, 3, 1, 2)):
        for j in range(4):
            piece, lower = pieces[2 * i + j // 2], 32 * (j % 2)
            rows = rows_at(place, step, j)
            gg[rows] = piece[0, lower : lower + 32, :]
            ug[rows] = piece[1, lower : lower + 32, :]


def give_kernel(place, gate, up, *refs):
    pieces, out, gg, ug = refs[:8], *refs[8:]
    assemble(place, pieces, gg, ug)
    out[...] = input_sum(gg[out.shape[0] :], ug[out.shape[0] :], gate, up).astype(BF16)


def input_sum(gg, ug, gate, up):
    contract = (((1,), (1,)), ((), ()))
    total = lax.dot_general(gg, gate[...], contract, preferred_element_type=F32)
    return total + lax.dot_general(ug, up[...], contract, preferred_element_type=F32)


def keep_kernel(gate, up, gg, ug, out):
    rows = out.shape[0]
    out[...] = input_sum(gg[:rows], ug[:rows], gate, up)


def feature_kernel(low, high, gg, ug, gate_out, up_out, act):
    width, rows = gate_out.shape[0], low.shape[0]
    act[:rows] = low[:, :width]
    act[rows:] = high[:, :width]
    contract = (((0,), (0,)), ((), ()))
    for grad, out in ((gg, gate_out), (ug, up_out)):
        out[...] = lax.dot_general(
            act[...], grad[...], contract, preferred_element_type=F32
        ).astype(BF16)


def hidden_kernel(place, low, high, *refs):
    pieces, down_out, act, hid = refs[:4], *refs[4:]
    for i, step in enumerate((0, 2, 3, 1)):
        for j in range(4):
            hid[rows_at(place, step, j)] = pieces[i][32 * j : 32 * j + 32]
    width, rows = down_out.shape[1], low.shape[0]
    act[:rows] = low[:, width:]
    act[rows:] = high[:, width:]
    contract = (((0,), (0,)), ((), ()))
    down_out[...] = lax.dot_general(
        hid[...], act[...], contract, preferred_element_type=F32
    ).astype(BF16)


def split_kernel(keep, got, *outs):
    count = outs[0].shape[0]
    for i in range(4):
        rows = slice(count * i, count * i + count)
        outs[i][...] = (keep[rows] + got[rows].astype(F32)).astype(BF16)


def sum_kernel(*refs):
    total = refs[0][...].astype(F32)
    for ref in refs[1:-1]:
        total = total + ref[...].astype(F32)
    refs[-1][...] = total.astype(BF16)


def merge_kernel(mine, got, out, held, sems):
    count = mine.shape[0] // MERGE
    copies = []
    for i in range(MERGE):
        rows = pl.ds(count * i, count)
        held[rows] = (mine[rows].astype(F32) + got[rows].astype(F32)).astype(BF16)
        copies.append(pltpu.make_async_copy(held.at[rows], out.at[rows], sems.at[i]))
        copies[-1].start()
    for copy in copies:
        copy.wait()


def merge(term):
    return pl.pallas_call(
        merge_kernel,
        out_shape=jax.ShapeDtypeStruct(term.shape, BF16),
        in_specs=[pl.BlockSpec(memory_space=pltpu.VMEM)] * 2,
        out_specs=pl.BlockSpec(memory_space=pl.ANY),
        scratch_shapes=[pltpu.VMEM(term.shape, BF16), pltpu.SemaphoreType.DMA((MERGE,))],
        compiler_params=pltpu.CompilerParams(vmem_limit_bytes=24 * 1024 * 1024),
    )(term, swap_dp(term))


def body(tokens, cotangent, gate, up, down):
    width, hidden = gate.shape
    count = tokens.shape[0]
    rows = 8 * count
    col, row, dp = lax.axis_index("col"), lax.axis_index("row"), lax.axis_index("dp")
    x, y = lax.rem(col, RING), lax.div(col, RING)
    here, other = jnp.where(dp == 0, x, y), jnp.where(dp == 0, y, x)
    place = jnp.stack([here, other]).astype(jnp.int32)

    mine = call(pack_kernel, [((count, 2 * width), BF16)], (tokens, cotangent))[0]
    evens = [mine] + [send_row(mine, -2 * i) for i in range(1, 4)]
    even = call(bundle_kernel, [((4 * count, 2 * width), BF16)], evens)[0]
    odd = swap_row(even)

    third, half = ((3, 32, hidden), BF16), ((3, 64, hidden), BF16)
    weights = (gate, up, down)

    def products(steps, kind, act, earlier):
        return call(
            functools.partial(product_kernel, steps),
            [kind] * (2 * len(steps)),
            (place, act) + weights + tuple(earlier),
            flops=2 * 64 * len(steps) * width * hidden * 3,
        )

    part = products((2, 1, 3, 0), third, even, ())
    part = products((2,), half, odd, part[:2]) + products((1, 3, 0), half, odd, part[2:])
    far_up, far_down, pass_up, near_up, near_down, pass_down, low, high = part
    far_up, far_down = send_col(far_up, 0, 1), send_col(far_down, 0, -1)
    near_up, near_down = send_col(near_up, 0, 1), send_col(near_down, 0, -1)
    relay = call(add_kernel, [half] * 2, (pass_up, pass_down, far_up, far_down))
    relay_up, relay_down = send_col(relay[0], 0, 1), send_col(relay[1], 0, -1)
    own = call(
        own_kernel,
        [third] * 4,
        (place, low, relay_up, near_down, high, relay_down, near_up),
        scratch=[pltpu.VMEM((4, 3, 32, hidden), BF16)],
    )
    got = [own[0]] + [send_col(own[step], 1, step) for step in STEPS]
    unit = call(unit_kernel, [third], got)[0]
    got = [unit] + [send_col(unit, 1, step) for step in STEPS]
    low, high, hid = call(
        join_kernel,
        [((2, 64, hidden), BF16)] * 2 + [((128, hidden), BF16)],
        got,
    )
    low_left, high_right = send_col(low, 0, 1), send_col(high, 0, -1)
    high_left, low_right = send_col(high, 0, 1), send_col(low, 0, -1)
    low_far, high_far = send_col(low_left, 0, 1), send_col(high_right, 0, -1)
    hid, high_left, low_right = lax.optimization_barrier((hid, high_left, low_right))
    pieces = (low, high, low_left, high_left, low_right, high_right, low_far, high_far)
    hids = (hid, *(send_col(hid, 0, step) for step in STEPS))

    whole = pltpu.VMEM((rows, hidden), BF16)
    lhs = pltpu.VMEM((rows, width), BF16)
    work = 2 * rows * width * hidden
    give, gg, ug = call(
        give_kernel,
        [((4 * count, width), BF16)] + [((rows, hidden), BF16)] * 2,
        (place, gate, up) + pieces,
        flops=work,
    )
    swapped = swap_row(give)
    keep = call(keep_kernel, [((4 * count, width), F32)], (gate, up, gg, ug), flops=work)[0]
    features = call(
        feature_kernel,
        [((width, hidden), BF16)] * 2,
        (even, odd, gg, ug),
        scratch=[lhs],
        flops=2 * work,
    )
    swapped, keep, *features = lax.optimization_barrier((swapped, keep, *features))
    block = ((count, width), BF16)
    sums = call(split_kernel, [block] * 4, (keep, swapped))
    sums, hids = lax.optimization_barrier((sums, hids))
    outs = [merge(term) for term in features]
    down_term = call(
        hidden_kernel,
        [((hidden, width), BF16)],
        (place, even, odd) + hids,
        scratch=[lhs, whole],
        flops=work,
    )[0]
    got = [sums[0]] + [send_row(sums[i], 2 * i) for i in range(1, 4)]
    got, outs = lax.optimization_barrier((got, outs))
    input_grad = call(sum_kernel, [block], got)[0]
    outs = list(outs) + [merge(down_term)]
    return (input_grad,) + tuple(outs)


def solution(mesh):
    placed = (
        P(("dp", "row"), "col"),
        P(("dp", "row"), "col"),
        P("col", "row"),
        P("col", "row"),
        P("row", "col"),
    )
    return jax.shard_map(
        body,
        mesh=mesh,
        in_specs=placed,
        out_specs=(P(("dp", "row"), "col"), P("col", "row"), P("col", "row"), P("row", "col")),
        check_vma=False,
    )
```

```python
import functools

import jax
import jax.numpy as jnp
from jax import lax
from jax.experimental import pallas as pl
from jax.experimental.pallas import tpu as pltpu
from jax.sharding import PartitionSpec as P

RING = 4
STEPS = (2, 1, 3)
MERGE = 8
BF16 = jnp.bfloat16
F32 = jnp.float32


def send_col(value, axis, step):
    pairs = []
    for dp in range(2):
        for y in range(RING):
            for x in range(RING):
                if axis ^ dp == 0:
                    to = y * RING + (x + step) % RING
                else:
                    to = ((y + step) % RING) * RING + x
                pairs.append((dp * 16 + y * RING + x, dp * 16 + to))
    return lax.ppermute(value, ("dp", "col"), pairs)


def send_row(value, step):
    pairs = []
    for dp in range(2):
        for row in range(8):
            to = (row + step if dp == 0 else row - step) % 8
            pairs.append((dp * 8 + row, dp * 8 + to))
    return lax.ppermute(value, ("dp", "row"), pairs)


def partner(dp, row):
    return (row + 1 if row % 2 == dp else row - 1) % 8


def swap_row(value):
    pairs = [(dp * 8 + row, dp * 8 + partner(dp, row)) for dp in range(2) for row in range(8)]
    return lax.ppermute(value, ("dp", "row"), pairs)


def swap_dp(value):
    return lax.ppermute(value, "dp", [(0, 1), (1, 0)])


def call(kernel, outs, args, scratch=(), flops=0, vmem=24, placed=True):
    whole = pl.BlockSpec(memory_space=pltpu.VMEM)
    small = pl.BlockSpec(memory_space=pltpu.SMEM)
    where = whole if placed else pl.BlockSpec(memory_space=pl.ANY)
    moved = sum(a.size * a.dtype.itemsize for a in args)
    return pl.pallas_call(
        kernel,
        out_shape=[jax.ShapeDtypeStruct(shape, kind) for shape, kind in outs],
        in_specs=[small if a.dtype == jnp.int32 else where for a in args],
        out_specs=[whole] * len(outs),
        scratch_shapes=list(scratch),
        compiler_params=pltpu.CompilerParams(vmem_limit_bytes=vmem * 1024 * 1024),
        cost_estimate=pl.CostEstimate(flops=flops, bytes_accessed=moved, transcendentals=0),
    )(*args)


def rows_of(start, count):
    return pl.ds(pl.multiple_of(start, 32), count)


def pack_kernel(tokens, cotangent, out):
    width = tokens.shape[1]
    out[:, :width] = tokens[...]
    out[:, width:] = cotangent[...]


def bundle_kernel(*refs):
    count = refs[0].shape[0]
    for i in range(4):
        refs[4][count * i : count * i + count] = refs[i][...]


def product_kernel(steps, place, act, gate, up, down, *refs):
    groups = 2 * len(steps)
    first, outs = refs[:-groups], refs[-groups:]
    width = gate.shape[0]
    rows = [rows_of(lax.rem(place[0] + step, RING) * 64, 64) for step in steps]
    both = jnp.concatenate([act[r] for r in rows], axis=0)
    tok, cot = both[:, :width], both[:, width:]
    for k in range(3):
        if k < 2:
            term = jnp.dot(tok, (gate, up)[k][...], preferred_element_type=F32)
        else:
            term = lax.dot_general(
                cot, down[...], (((1,), (1,)), ((), ())), preferred_element_type=F32
            )
        term = term.astype(BF16)
        for q in range(groups):
            out = outs[q]
            out[k, out.shape[1] - 32 :] = term[32 * q : 32 * q + 32]
    if first:
        for q in range(groups):
            outs[q][:, :32] = first[q][...]


def add_kernel(*refs):
    count = len(refs) // 3
    for i in range(count):
        total = refs[i][...].astype(F32) + refs[count + i][...].astype(F32)
        refs[2 * count + i][...] = total.astype(BF16)


def own_kernel(place, *refs):
    got, outs, held = refs[:6], refs[6:10], refs[10]
    for part in range(2):
        mine, relay, near = got[3 * part : 3 * part + 3]
        total = mine[...].astype(F32) + relay[...].astype(F32) + near[...].astype(F32)
        total = total.astype(BF16)
        held[part] = total[:, :32]
        held[2 + part] = total[:, 32:]
    for step in range(RING):
        outs[step][...] = held[lax.rem(place[1] + step, RING)]


def unit_kernel(own, one, two, three, out):
    gate_sum, up_sum, back_sum = (
        own[k].astype(F32) + one[k].astype(F32) + two[k].astype(F32) + three[k].astype(F32)
        for k in range(3)
    )
    sig = jax.nn.sigmoid(gate_sum)
    silu = gate_sum * sig
    out[0] = (back_sum * up_sum * sig * (1.0 + gate_sum * (1.0 - sig))).astype(BF16)
    out[1] = (back_sum * silu).astype(BF16)
    out[2] = (silu * up_sum).astype(BF16)


def join_kernel(*refs):
    low, high, hid = refs[4:]
    for j, ref in zip((0,) + STEPS, refs):
        rows = slice(32 * (j % 2), 32 * (j % 2) + 32)
        (low if j < 2 else high)[:, rows] = ref[:2]
        hid[32 * j : 32 * j + 32] = ref[2]


def rows_at(place, step, j):
    block = lax.rem(place[0] + step, RING)
    sub = lax.rem(place[1] + RING - j, RING)
    return rows_of(256 * lax.div(sub, 2) + 64 * block + 32 * lax.rem(sub, 2), 32)


def assemble(place, pieces, gg, ug):
    for i, step in enumerate((0, 3, 1, 2)):
        for j in range(4):
            piece, lower = pieces[2 * i + j // 2], 32 * (j % 2)
            rows = rows_at(place, step, j)
            gg[rows] = piece[0, lower : lower + 32, :]
            ug[rows] = piece[1, lower : lower + 32, :]


def give_kernel(place, gate, up, *refs):
    pieces, out, gg, ug = refs[:8], *refs[8:]
    assemble(place, pieces, gg, ug)
    out[...] = input_sum(gg[out.shape[0] :], ug[out.shape[0] :], gate, up).astype(BF16)


def input_sum(gg, ug, gate, up):
    contract = (((1,), (1,)), ((), ()))
    total = lax.dot_general(gg, gate[...], contract, preferred_element_type=F32)
    return total + lax.dot_general(ug, up[...], contract, preferred_element_type=F32)


def keep_kernel(gate, up, gg, ug, out):
    rows = out.shape[0]
    out[...] = input_sum(gg[:rows], ug[:rows], gate, up)


def feature_kernel(low, high, gg, ug, gate_out, up_out, act):
    width, rows = gate_out.shape[0], low.shape[0]
    act[:rows] = low[:, :width]
    act[rows:] = high[:, :width]
    contract = (((0,), (0,)), ((), ()))
    for grad, out in ((gg, gate_out), (ug, up_out)):
        out[...] = lax.dot_general(
            act[...], grad[...], contract, preferred_element_type=F32
        ).astype(BF16)


def hidden_kernel(place, low, high, *refs):
    pieces, down_out, act, hid = refs[:4], *refs[4:]
    for i, step in enumerate((0, 2, 3, 1)):
        for j in range(4):
            hid[rows_at(place, step, j)] = pieces[i][32 * j : 32 * j + 32]
    width, rows = down_out.shape[1], low.shape[0]
    act[:rows] = low[:, width:]
    act[rows:] = high[:, width:]
    contract = (((0,), (0,)), ((), ()))
    down_out[...] = lax.dot_general(
        hid[...], act[...], contract, preferred_element_type=F32
    ).astype(BF16)


def split_kernel(keep, got, *outs):
    count = outs[0].shape[0]
    for i in range(4):
        rows = slice(count * i, count * i + count)
        outs[i][...] = (keep[rows] + got[rows].astype(F32)).astype(BF16)


def sum_kernel(*refs):
    total = refs[0][...].astype(F32)
    for ref in refs[1:-1]:
        total = total + ref[...].astype(F32)
    refs[-1][...] = total.astype(BF16)


def merge_kernel(mine, got, out, held, sems):
    count = mine.shape[0] // MERGE
    copies = []
    for i in range(MERGE):
        rows = pl.ds(count * i, count)
        held[rows] = (mine[rows].astype(F32) + got[rows].astype(F32)).astype(BF16)
        copies.append(pltpu.make_async_copy(held.at[rows], out.at[rows], sems.at[i]))
        copies[-1].start()
    for copy in copies:
        copy.wait()


def merge(term):
    return pl.pallas_call(
        merge_kernel,
        out_shape=jax.ShapeDtypeStruct(term.shape, BF16),
        in_specs=[pl.BlockSpec(memory_space=pltpu.VMEM)] * 2,
        out_specs=pl.BlockSpec(memory_space=pl.ANY),
        scratch_shapes=[pltpu.VMEM(term.shape, BF16), pltpu.SemaphoreType.DMA((MERGE,))],
        compiler_params=pltpu.CompilerParams(vmem_limit_bytes=24 * 1024 * 1024),
    )(term, swap_dp(term))


def body(tokens, cotangent, gate, up, down):
    width, hidden = gate.shape
    count = tokens.shape[0]
    rows = 8 * count
    col, row, dp = lax.axis_index("col"), lax.axis_index("row"), lax.axis_index("dp")
    x, y = lax.rem(col, RING), lax.div(col, RING)
    here, other = jnp.where(dp == 0, x, y), jnp.where(dp == 0, y, x)
    place = jnp.stack([here, other]).astype(jnp.int32)

    mine = call(pack_kernel, [((count, 2 * width), BF16)], (tokens, cotangent))[0]
    evens = {i: send_row(mine, -2 * i) for i in STEPS}
    evens = (mine, evens[1], evens[2], evens[3])
    even = call(bundle_kernel, [((4 * count, 2 * width), BF16)], evens)[0]
    odd = swap_row(even)

    third, half = ((3, 32, hidden), BF16), ((3, 64, hidden), BF16)
    weights = (gate, up, down)

    def products(steps, kind, act, earlier):
        return call(
            functools.partial(product_kernel, steps),
            [kind] * (2 * len(steps)),
            (place, act) + weights + tuple(earlier),
            flops=2 * 64 * len(steps) * width * hidden * 3,
        )

    part = products((2, 1, 3, 0), third, even, ())
    part = products((2,), half, odd, part[:2]) + products((1, 3, 0), half, odd, part[2:])
    far_up, far_down, pass_up, near_up, near_down, pass_down, low, high = part
    far_up, far_down = send_col(far_up, 0, 1), send_col(far_down, 0, -1)
    near_up, near_down = send_col(near_up, 0, 1), send_col(near_down, 0, -1)
    relay = call(add_kernel, [half] * 2, (pass_up, pass_down, far_up, far_down))
    relay_up, relay_down = send_col(relay[0], 0, 1), send_col(relay[1], 0, -1)
    own = call(
        own_kernel,
        [third] * 4,
        (place, low, relay_up, near_down, high, relay_down, near_up),
        scratch=[pltpu.VMEM((4, 3, 32, hidden), BF16)],
    )
    got = [own[0]] + [send_col(own[step], 1, step) for step in STEPS]
    unit = call(unit_kernel, [third], got)[0]
    got = [unit] + [send_col(unit, 1, step) for step in STEPS]
    low, high, hid = call(
        join_kernel,
        [((2, 64, hidden), BF16)] * 2 + [((128, hidden), BF16)],
        got,
    )
    low_left, high_right = send_col(low, 0, 1), send_col(high, 0, -1)
    high_left, low_right = send_col(high, 0, 1), send_col(low, 0, -1)
    low_far, high_far = send_col(low_left, 0, 1), send_col(high_right, 0, -1)
    hid, high_left, low_right = lax.optimization_barrier((hid, high_left, low_right))
    pieces = (low, high, low_left, high_left, low_right, high_right, low_far, high_far)
    hids = (hid, *(send_col(hid, 0, step) for step in STEPS))

    whole = pltpu.VMEM((rows, hidden), BF16)
    lhs = pltpu.VMEM((rows, width), BF16)
    work = 2 * rows * width * hidden
    give, gg, ug = call(
        give_kernel,
        [((4 * count, width), BF16)] + [((rows, hidden), BF16)] * 2,
        (place, gate, up) + pieces,
        flops=work,
    )
    swapped = swap_row(give)
    keep = call(keep_kernel, [((4 * count, width), F32)], (gate, up, gg, ug), flops=work)[0]
    features = call(
        feature_kernel,
        [((width, hidden), BF16)] * 2,
        (even, odd, gg, ug),
        scratch=[lhs],
        flops=2 * work,
    )
    swapped, keep, *features = lax.optimization_barrier((swapped, keep, *features))
    block = ((count, width), BF16)
    sums = call(split_kernel, [block] * 4, (keep, swapped))
    sums, hids = lax.optimization_barrier((sums, hids))
    outs = [merge(term) for term in features]
    down_term = call(
        hidden_kernel,
        [((hidden, width), BF16)],
        (place, even, odd) + hids,
        scratch=[lhs, whole],
        flops=work,
    )[0]
    got = [sums[0]] + [send_row(sums[i], 2 * i) for i in STEPS]
    got, outs = lax.optimization_barrier((got, outs))
    input_grad = call(sum_kernel, [block], got)[0]
    outs = list(outs) + [merge(down_term)]
    return (input_grad,) + tuple(outs)


def solution(mesh):
    placed = (
        P(("dp", "row"), "col"),
        P(("dp", "row"), "col"),
        P("col", "row"),
        P("col", "row"),
        P("row", "col"),
    )
    return jax.shard_map(
        body,
        mesh=mesh,
        in_specs=placed,
        out_specs=(P(("dp", "row"), "col"), P("col", "row"), P("col", "row"), P("row", "col")),
        check_vma=False,
    )
```
